32 devices in a mesh: groups: 2 (over x), ctx: 16 (over z, y, core).
Axes of the slice: x: 2, y: 2, z: 4, core: 2. Of those that a mesh axis runs over, the one named last changes fastest.
Arguments:
- queries: bfloat16 [4096, 36864], P(('groups', 'ctx')), parts along dimension 0, may hold values from -48 to 48
- kv_cache: bfloat16 [4096, 576], P(('groups', 'ctx')), parts along dimension 0, may hold values from -4 to 4
- idx_queries: bfloat16 [4096, 4096], P(('groups', 'ctx')), parts along dimension 0, may hold values from -5 to 5
- idx_keys: bfloat16 [4096, 128], P(('groups', 'ctx')), parts along dimension 0, may hold values from -12 to 12
- idx_weights: float32 [4096, 32], P(('groups', 'ctx')), parts along dimension 0, may hold values from -1 to 1
- selected: int32 [4096, 2], P(('groups', 'ctx')), parts along dimension 0, may hold values from 0 to 15, as said below
- value_maps: bfloat16 [64, 512, 128], P('ctx'), may hold values from -0.25 to 0.25
Outputs:
- attended: bfloat16 [4096, 8192], P(('groups', 'ctx')), parts along dimension 0
- index_scores: float32 [4096, 16], P(('groups', 'ctx')), parts along dimension 0
The draws below stay inside these ranges and needn't reach their ends.
There are 2 independent parts, one for each index of `groups`. The reference program is written for one: setup_inputs(seed, part) draws one part's arguments, and reference() takes and returns one part's arrays. A program takes and returns all parts, laid end to end along the dimension named above; an argument that names none is the same for every part. Nothing has to cross between parts.
Inputs may be any that keep to these rules, and one draw needn't show every extreme that they name: selected[t, 0] = t // 128; for 1 <= k <= t // 128, slot k names a block below t // 128, all of them distinct; slots k > t // 128 hold block numbers that are not used.
All inputs are finite; a program needn't handle non-finite values.
Results may differ from the reference program's by a relative error of at most 0.0058.
Values may be sent and summed in bfloat16 or wider, within the bound.
No kernel may reach another device: no remote copies, remote signals or barrier semaphores. Data moves between devices by JAX's collectives and lax.ppermute only.
A program may use at most 384 MiB of HBM per device.

```python
import math
import jax
import jax.numpy as jnp
from jax import lax

H = 64
DL = 512
DR = 64
DV = 128
HI = 32
DI = 128
BLK = 128
TOPB = 2
TOKENS = 2048
NB = 16


def latent_rows(key):
    return jnp.clip(jax.random.normal(key, (TOKENS, DL + DR), jnp.float32), -4.0, 4.0)


def draw_kv_cache(key, part):
    shared_rows = latent_rows(key)
    return shared_rows.astype(jnp.bfloat16)


def draw_queries(key, part):
    key = jax.random.fold_in(key, 12)
    fresh = jnp.clip(jax.random.normal(key, (TOKENS, H, DL + DR), jnp.float32), -4.0, 4.0)
    return fresh.reshape(TOKENS, H * (DL + DR)).astype(jnp.bfloat16)


def draw_idx_keys(key, part):
    key = jax.random.fold_in(key, 13)
    first_key, second_key = jax.random.split(key, 2)
    spread = jnp.exp(jax.random.uniform(first_key, (TOKENS, 1), jnp.float32, jnp.log(0.3), jnp.log(3.0)))
    return (spread * jnp.clip(jax.random.normal(second_key, (TOKENS, DI), jnp.float32), -4.0, 4.0)).astype(jnp.bfloat16)


def draw_selected(key, part):
    key = jax.random.fold_in(key, 21)
    ranking = jax.random.randint(key, (TOKENS, NB), 0, 1 << 20, jnp.int32)
    columns = jnp.arange(NB, dtype=jnp.int32)[None, :]
    own_block = (jnp.arange(TOKENS, dtype=jnp.int32) // BLK)[:, None]
    ordered = jnp.where(columns < own_block, ranking * NB + columns, -1 - columns)
    unused, picked = lax.top_k(ordered, TOPB - 1)
    return jnp.concatenate([own_block, picked.astype(jnp.int32)], axis=1).astype(jnp.int32)


def shard_levels(rng, dims, shards, least, top_value):
    loudness, own = 1.0, jax.random.fold_in(rng, 6)
    for position, blocks in shards:
        draws = jnp.exp(jax.random.uniform(jax.random.fold_in(own, position), (blocks,), jnp.float32, least / len(shards), top_value / len(shards)))
        loudness = loudness * jnp.repeat(draws, dims[position] // blocks).reshape([-1 if axis == position else 1 for axis in range(len(dims))])
    return loudness


def gaussian(own_key, dims, scale, bound, shards=(), kind=jnp.bfloat16):
    values = jax.random.normal(own_key, dims, jnp.float32) * scale
    if len(shards) > 0:
        values = shard_levels(own_key, dims, shards, -0.22, 0.18) * values
    return jnp.clip(values, min=-bound, max=bound).astype(kind)


def setup_inputs(seed: int = 0, part: int = 0) -> dict:
    keys = jax.random.split(jax.random.key(seed), 8)
    part_keys = jax.random.split(jax.random.fold_in(keys[7], part), 8)
    return {
        "queries": draw_queries(jax.random.fold_in(jax.random.fold_in(keys[7], part), 71), part),
        "kv_cache": draw_kv_cache(jax.random.fold_in(jax.random.fold_in(keys[7], part), 71), part),
        "idx_queries": gaussian(part_keys[2], (TOKENS, HI * DI), 1.0, 5.0, ((0, 16),)),
        "idx_keys": draw_idx_keys(jax.random.fold_in(jax.random.fold_in(keys[7], part), 71), part),
        "idx_weights": gaussian(part_keys[4], (TOKENS, HI), HI ** -0.5, 1.0, ((0, 16),), jnp.float32),
        "selected": draw_selected(jax.random.fold_in(jax.random.fold_in(keys[7], part), 71), part),
        "value_maps": gaussian(keys[6], (H, DL, DV), DL ** -0.5, 0.25, ((0, 16),)),
    }


score_scale = 192.0 ** -0.5


def block_scores(query_rows, weight_rows, row_pos, idx_keys):
    count = query_rows.shape[0]
    logits = jnp.dot(query_rows.reshape(count * HI, DI), idx_keys.T, preferred_element_type=jnp.float32).astype(jnp.bfloat16)
    active = jnp.maximum(logits.astype(jnp.float32), 0.0).reshape(count, HI, idx_keys.shape[0])
    relevance = jnp.einsum('rh,rhk->rk', weight_rows, active, precision=lax.Precision.HIGHEST) * (DI ** -0.5)
    key_pos = jnp.arange(idx_keys.shape[0], dtype=jnp.int32)
    relevance = jnp.where(key_pos[None, :] <= row_pos[:, None], relevance, 0.0)
    onehot = (key_pos[:, None] // BLK == jnp.arange(NB, dtype=jnp.int32)[None, :]).astype(jnp.float32)
    sums = jnp.dot(relevance, onehot, precision=lax.Precision.HIGHEST)
    counts = jnp.clip(row_pos[:, None] - BLK * jnp.arange(NB, dtype=jnp.int32)[None, :] + 1, 0, BLK).astype(jnp.float32)
    return sums / jnp.maximum(counts, 1.0)


def reference(queries, kv_cache, idx_queries, idx_keys, idx_weights, selected, value_maps):
    positions = jnp.arange(TOKENS, dtype=jnp.int32)
    step_rows = math.gcd(128, TOKENS)

    def score_rows(inputs):
        query_rows, weight_rows, row_pos = inputs
        return block_scores(query_rows, weight_rows, row_pos, idx_keys)

    index_scores = lax.map(score_rows, (idx_queries.reshape(-1, step_rows, HI * DI), idx_weights.reshape(-1, step_rows, HI), positions.reshape(-1, step_rows))).reshape(TOKENS, NB)
    group_size = math.gcd(16, TOKENS)

    def attend(inputs):
        query_rows, chosen, row_pos = inputs
        key_pos = chosen[:, :, None] * BLK + jnp.arange(BLK, dtype=jnp.int32)[None, None, :]
        slot_ok = jnp.arange(TOPB, dtype=jnp.int32)[None, :, None] <= (row_pos // BLK)[:, None, None]
        usable = (slot_ok & (key_pos <= row_pos[:, None, None])).reshape(group_size, TOPB * BLK)
        key_rows = kv_cache[key_pos.reshape(group_size, TOPB * BLK)]
        scores = jnp.einsum('ghd,gkd->ghk', query_rows.astype(jnp.float32), key_rows.astype(jnp.float32)) * score_scale
        scores = jnp.where(usable[:, None, :], scores, -jnp.inf)
        row_max = jnp.max(scores, axis=-1, keepdims=True)
        expd = jnp.exp(scores - row_max)
        weights = (expd / jnp.sum(expd, axis=-1, keepdims=True)).astype(jnp.bfloat16)
        latent_out = jnp.einsum('ghk,gkd->ghd', weights.astype(jnp.float32), key_rows[:, :, :DL].astype(jnp.float32)).astype(jnp.bfloat16)
        return jnp.einsum('ghd,hde->ghe', latent_out.astype(jnp.float32), value_maps.astype(jnp.float32)).astype(jnp.bfloat16)

    attended = lax.map(attend, (queries.reshape(-1, group_size, H, DL + DR), selected.reshape(-1, group_size, TOPB), positions.reshape(-1, group_size))).reshape(TOKENS, H * DV)
    return attended, index_scores
```

```python
import functools
import math

import jax
import jax.numpy as jnp
from jax import lax
from jax.experimental import pallas as pl
from jax.experimental.pallas import tpu as pltpu
from jax.sharding import PartitionSpec as P

H = 64
DL = 512
DR = 64
DV = 128
HI = 32
DI = 128
BLK = 128
WIN = 16
DQ = DL + DR
PACK = DI + DQ

exponent_scale = 192.0 ** (-0.5) * math.log2(math.e)
f32 = jnp.float32
bf16 = jnp.bfloat16
SMALL = pl.CostEstimate(flops=1, bytes_accessed=1, transcendentals=0)


def sort_kernel(order_ref, q_ref, out_ref):
    heads = out_ref.shape[1]
    windows = out_ref.shape[0]
    rows = jnp.dot(order_ref[...], q_ref[...], preferred_element_type=f32)
    for h in range(heads):
        part = rows[:, h * DQ : (h + 1) * DQ].astype(bf16)
        out_ref[:, h] = part.reshape(windows, WIN, DQ)


def sort_queries(order, queries):
    count = queries.shape[0]
    step = 16
    return pl.pallas_call(
        sort_kernel,
        grid=(H // step,),
        in_specs=[
            pl.BlockSpec((count, count), lambda i: (0, 0)),
            pl.BlockSpec((count, step * DQ), lambda i: (0, i)),
        ],
        out_specs=pl.BlockSpec((count // WIN, step, WIN, DQ), lambda i: (0, i, 0, 0)),
        out_shape=jax.ShapeDtypeStruct((count // WIN, H, WIN, DQ), bf16),
        compiler_params=pltpu.CompilerParams(vmem_limit_bytes=48 * 2**20),
        cost_estimate=SMALL,
        name="sort_queries",
    )(order, queries)


def with_block(pieces, place, use):
    size = pieces[0].shape[0]
    if len(pieces) == 1:
        use(pieces[0].at[place])
        return
    for k, piece in enumerate(pieces):

        @pl.when(place // size == k)
        def _():
            use(piece.at[lax.rem(place, size)])


def place_of(relative, j, me):
    if not relative:
        return j
    other = j ^ me
    return (other & 1) * 8 + ((other >> 1) & 1) * 4 + (other >> 2)


def attend_kernel(relative, count, first_ref, key_ref, me_ref, q_ref, pos_ref, keys_ref, *refs):
    pieces = refs[:count]
    out_ref, rhs_ref = refs[count:]
    w = pl.program_id(0)
    me = me_ref[0]
    lo = w * WIN

    def load(j, column):
        def use(block):
            rhs_ref[:, column : column + BLK] = block[DI:PACK, :]

        with_block(pieces, place_of(relative, j, me), use)

    @pl.when(w == 0)
    def _():
        load(me, 0)

    column = lax.broadcasted_iota(jnp.int32, (WIN, 2 * BLK), 1)
    last = jnp.where(me > 0, 2 * BLK, 0)
    usable = (column <= pos_ref[...]) | ((column >= BLK) & (column < last))
    bias = jnp.where(usable, 0.0, -jnp.inf).astype(f32)
    keys = keys_ref[...]

    def block(j, carry):
        start = jnp.maximum(first_ref[j], lo)
        end = jnp.minimum(first_ref[j + 1], lo + WIN)

        @pl.when(end > start)
        def _():
            load(j, BLK)
            mine = (keys == j)[None]
            scores = jnp.dot(
                q_ref[0].reshape(H * WIN, DQ), rhs_ref[...], preferred_element_type=f32
            ).reshape(H, WIN, 2 * BLK) + bias[None]
            top = jnp.max(scores, axis=-1, keepdims=True)
            expd = jnp.exp2((scores - top) * exponent_scale)
            total = jnp.sum(expd, axis=-1, keepdims=True)
            weights = (expd * (1.0 / total)).astype(bf16)
            values = lax.dot_general(
                weights.reshape(H * WIN, 2 * BLK),
                rhs_ref[0:DL, :],
                (((1,), (1,)), ((), ())),
                preferred_element_type=f32,
            ).reshape(H, WIN, DL)
            old = out_ref[...].astype(f32)
            out_ref[...] = jnp.where(mine, values, old).astype(bf16)

        return carry

    lax.fori_loop(key_ref[lo], key_ref[lo + WIN - 1] + 1, block, 0)


def attend(relative, first, sorted_key, me, sorted_q, pieces, sorted_pos):
    count = sorted_key.shape[0]
    spec = pltpu.PrefetchScalarGridSpec(
        num_scalar_prefetch=3,
        grid=(count // WIN,),
        in_specs=[
            pl.BlockSpec((1, H, WIN, DQ), lambda w, *_: (w, 0, 0, 0)),
            pl.BlockSpec((WIN, 1), lambda w, *_: (w, 0)),
            pl.BlockSpec((WIN, 1), lambda w, *_: (w, 0)),
        ]
        + [pl.BlockSpec((p.shape[0], PACK, BLK), lambda w, *_: (0, 0, 0)) for p in pieces],
        out_specs=pl.BlockSpec((H, WIN, DL), lambda w, *_: (0, w, 0)),
        scratch_shapes=[pltpu.VMEM((DQ, 2 * BLK), bf16)],
    )
    return pl.pallas_call(
        functools.partial(attend_kernel, relative, len(pieces)),
        grid_spec=spec,
        out_shape=jax.ShapeDtypeStruct((H, count, DL), bf16),
        compiler_params=pltpu.CompilerParams(vmem_limit_bytes=48 * 2**20),
        cost_estimate=SMALL,
        name="attend",
    )(first, sorted_key, me, sorted_q, sorted_pos[:, None], sorted_key[:, None], *pieces)


def unit_place(unit, me_ref):
    device, half, relative = unit
    side = (me_ref[1] ^ half) if relative else half
    return (me_ref[0] ^ device) * 2 + side


def project_kernel(units, sizes, before_units, final, me_ref, *refs):
    back_ref = refs[0]
    latents = refs[1 : 1 + len(units)]
    pieces = refs[1 + len(units) : 1 + len(units) + len(sizes)]
    out_ref = refs[-1]
    if before_units:
        before_ref = refs[-2]
        for n, unit in enumerate(before_units):
            place = pl.multiple_of(unit_place(unit, me_ref) * 2 * DV, 2 * DV)
            out_ref[:, pl.ds(place, 2 * DV)] = before_ref[:, n * 2 * DV : (n + 1) * 2 * DV]
    n = 0
    parts = []
    for piece, size in zip(pieces, sizes):
        for k in range(size):
            parts.append(
                jnp.dot(latents[n // 2][n % 2], piece[k], preferred_element_type=f32).astype(bf16)
            )
            n += 1
    rows = jnp.dot(
        back_ref[...], jnp.concatenate(parts, axis=1), preferred_element_type=f32
    ).astype(bf16)
    if not final:
        out_ref[...] = rows
        return
    for n, unit in enumerate(units):
        place = pl.multiple_of(unit_place(unit, me_ref) * 2 * DV, 2 * DV)
        out_ref[:, pl.ds(place, 2 * DV)] = rows[:, n * 2 * DV : (n + 1) * 2 * DV]


def project(me, back, latents, units, pieces, before_units=(), before=None, final=False):
    count = latents.shape[1]
    sizes = tuple(p.shape[0] for p in pieces)
    width = H * DV if final else len(units) * 2 * DV

    def latent_spec(unit):
        return pl.BlockSpec((2, count, DL), lambda i, me_ref: (unit_place(unit, me_ref), 0, 0))

    in_specs = [pl.BlockSpec((count, count), lambda i, m: (0, 0))]
    in_specs += [latent_spec(unit) for unit in units]
    in_specs += [pl.BlockSpec((n, DL, DV), lambda i, m: (0, 0, 0)) for n in sizes]
    operands = [me, back] + [latents] * len(units) + list(pieces)
    if before is not None:
        in_specs.append(pl.BlockSpec(before.shape, lambda i, m: (0, 0)))
        operands.append(before)
    spec = pltpu.PrefetchScalarGridSpec(
        num_scalar_prefetch=1,
        grid=(1,),
        in_specs=in_specs,
        out_specs=pl.BlockSpec((count, width), lambda i, m: (0, 0)),
    )
    return pl.pallas_call(
        functools.partial(project_kernel, tuple(units), sizes, tuple(before_units), final),
        grid_spec=spec,
        out_shape=jax.ShapeDtypeStruct((count, width), bf16),
        compiler_params=pltpu.CompilerParams(vmem_limit_bytes=56 * 2**20),
        cost_estimate=SMALL,
        name="project",
    )(*operands)


def index_kernel(relative, count, me_ref, q_ref, w_ref, *refs):
    pieces = refs[:count]
    out_ref, acc_ref, keys_ref = refs[count:]
    me = me_ref[0]
    rows = q_ref.shape[0]
    acc_ref[...] = jnp.zeros_like(acc_ref)
    row = lax.broadcasted_iota(jnp.int32, (BLK, rows), 0)
    col = lax.broadcasted_iota(jnp.int32, (BLK, rows), 1)

    def block(j, mask):
        def use(piece):
            keys_ref[...] = piece[...]

        with_block(pieces, place_of(relative, j, me), use)
        keys = keys_ref[...]
        total = jnp.zeros((8, rows), f32)
        for h in range(0, HI, 2):
            pair = jnp.concatenate(
                [q_ref[:, h * DI : (h + 1) * DI], q_ref[:, (h + 1) * DI : (h + 2) * DI]], axis=0
            )
            logits = lax.dot_general(keys, pair, (((1,), (1,)), ((), ())), preferred_element_type=f32)
            active = jnp.maximum(logits, 0.0)
            for k in range(2):
                half = active[:, k * rows : (k + 1) * rows]
                if mask is not None:
                    half = jnp.where(mask, half, 0.0)
                sums = jnp.sum(half.reshape(BLK // 8, 8, rows), axis=0)
                total = total + sums * w_ref[h + k : h + k + 1, :]
        acc_ref[pl.ds(j, 1), :] = jnp.sum(total, axis=0, keepdims=True)

    def step(j, carry):
        block(j, None)
        return carry

    lax.fori_loop(0, me, step, 0)
    block(me, row <= col)
    blocks = out_ref.shape[1]
    sums = acc_ref[...].T[:, 0:blocks]
    position = me * BLK + lax.broadcasted_iota(jnp.int32, (rows, blocks), 0)
    block_first = BLK * lax.broadcasted_iota(jnp.int32, (rows, blocks), 1)
    counts = jnp.clip(position - block_first + 1, 1, BLK).astype(f32)
    out_ref[...] = sums * (DI ** (-0.5)) / counts


def index_scores(relative, me, idx_queries, weights_t, pieces):
    count = idx_queries.shape[0]
    blocks = sum(p.shape[0] for p in pieces)
    rows = -(-blocks // 128) * 128
    spec = pltpu.PrefetchScalarGridSpec(
        num_scalar_prefetch=1,
        grid=(1,),
        in_specs=[
            pl.BlockSpec((count, HI * DI), lambda i, *_: (0, 0)),
            pl.BlockSpec((HI, count), lambda i, *_: (0, 0)),
        ]
        + [pl.BlockSpec((p.shape[0], BLK, DI), lambda i, *_: (0, 0, 0)) for p in pieces],
        out_specs=pl.BlockSpec((count, blocks), lambda i, *_: (0, 0)),
        scratch_shapes=[pltpu.VMEM((rows, count), f32), pltpu.VMEM((BLK, DI), bf16)],
    )
    return pl.pallas_call(
        functools.partial(index_kernel, relative, len(pieces)),
        grid_spec=spec,
        out_shape=jax.ShapeDtypeStruct((count, blocks), f32),
        compiler_params=pltpu.CompilerParams(vmem_limit_bytes=48 * 2**20),
        cost_estimate=SMALL,
        name="index_scores",
    )(me, idx_queries, weights_t, *pieces)


def on_ctx(me_to, devices=16):
    return [(i, me_to(i)) for i in range(devices)]


def over_z(k):
    return on_ctx(lambda i: i ^ (4 * k))


OVER_Y = on_ctx(lambda i: i ^ 2)
OVER_CORE = on_ctx(lambda i: i ^ 1)
OVER_XY = [(g * 16 + i, (1 - g) * 16 + (i ^ 2)) for g in range(2) for i in range(16)]


def along(array, pairs):
    return lax.ppermute(array, "ctx", pairs)


def after(array, *others):
    return lax.optimization_barrier((array,) + others)[0]


def on_device(queries, kv_cache, idx_queries, idx_keys, idx_weights, selected, value_maps):
    count = queries.shape[0]
    devices = lax.axis_size("ctx")
    blocks = count * devices // BLK
    assert count == BLK
    me = lax.axis_index("ctx")
    x = lax.axis_index("groups")
    meta = jnp.stack([me, x]).astype(jnp.int32)
    pack = jnp.concatenate([idx_keys, kv_cache.T], axis=0)
    relative = devices == 16 and lax.axis_size("groups") == 2 and value_maps.shape[0] == 4

    if relative:
        half = lax.dynamic_slice_in_dim(value_maps, 2 * x, 2, 0)
        pack_1, pack_2 = along(pack, over_z(1)), along(pack, over_z(2))
        half_1, half_2 = along(half, over_z(1)), along(half, over_z(2))
        from_y = along(value_maps, OVER_Y)
        pack_3 = along(pack_2, over_z(1))
        column_parts = [pack, pack_1, pack_2, pack_3]

    key = jnp.where(me > 0, selected[:, 1], 0)
    token = jnp.arange(count, dtype=jnp.int32)
    before = (key[:, None] < key[None, :]) | ((key[:, None] == key[None, :]) & (token[:, None] < token[None, :]))
    rank = jnp.sum(before.astype(jnp.int32), axis=0)
    order = rank[None, :] == token[:, None]
    back = order.T.astype(bf16)
    sorted_key = jnp.sum(jnp.where(order, key[None, :], 0), axis=1)
    sorted_pos = jnp.sum(jnp.where(order, token[None, :], 0), axis=1)
    first = jnp.sum(
        (key[None, :] < jnp.arange(blocks + 1, dtype=jnp.int32)[:, None]).astype(jnp.int32), axis=1
    )
    order = order.astype(bf16)
    if relative:
        order = after(order, pack_2)
    sorted_q = sort_queries(order, queries)

    if not relative:
        cache = lax.all_gather(pack, "ctx", axis=0, tiled=True).reshape(blocks, PACK, BLK)
        maps = lax.all_gather(value_maps, "ctx", axis=0, tiled=True)
        scores = index_scores(False, meta, idx_queries, idx_weights.T, [cache])
        latents = attend(False, first, sorted_key, meta, sorted_q, [cache], sorted_pos)
        meta = jnp.zeros_like(meta)
        parts = []
        for h in range(0, H, 16):
            units = [(u // 2, u % 2, False) for u in range(h // 2, h // 2 + 8)]
            parts.append(project(meta, back, latents, units, [maps[h : h + 16]]))
        return (jnp.concatenate(parts, axis=1), scores)

    half_3 = along(half_2, over_z(1))
    quarter_parts = [half_1, half_2, half_3]
    column = after(jnp.concatenate(column_parts, axis=0), sorted_q, half_2)
    column_y = along(column, OVER_Y)
    quarter = jnp.concatenate(quarter_parts, axis=0)
    quarter_x = lax.ppermute(quarter, "groups", [(0, 1), (1, 0)])
    quarter_y = along(quarter, OVER_Y)
    quarter_xy = lax.ppermute(quarter, ("groups", "ctx"), OVER_XY)
    pieces = [column, column_y, along(column, OVER_CORE), along(column_y, OVER_CORE)]
    pieces = [p.reshape(4, PACK, BLK) for p in pieces]
    pieces, quarter = lax.optimization_barrier((pieces, quarter))

    latents = attend(True, first, sorted_key, meta, sorted_q, pieces, sorted_pos)
    scores = index_scores(True, meta, idx_queries, idx_weights.T, pieces)

    def both_cores(arrays, units):
        arrays = list(arrays) + [along(a, OVER_CORE) for a in arrays]
        return arrays, units + [(device ^ 1, half, rel) for device, half, rel in units]

    early, early_units = both_cores(
        [value_maps, from_y, quarter],
        [(0, 0, False), (0, 1, False), (2, 0, False), (2, 1, False)] + [(4 * z, 0, True) for z in (1, 2, 3)],
    )
    early_out = project(meta, back, latents, early_units, early)
    late_in = [after(a, early_out) for a in (quarter_x, quarter_y, quarter_xy)]
    late, late_units = both_cores(
        late_in,
        [(4 * z, 1, True) for z in (1, 2, 3)]
        + [(4 * z + 2, 0, True) for z in (1, 2, 3)]
        + [(4 * z + 2, 1, True) for z in (1, 2, 3)],
    )
    attended = project(meta, back, latents, late_units, late, early_units, early_out, final=True)
    return (attended, scores)


def solution(mesh):
    return jax.shard_map(
        on_device,
        mesh=mesh,
        in_specs=(
            P(("groups", "ctx"), None),
            P(("groups", "ctx"), None),
            P(("groups", "ctx"), None),
            P(("groups", "ctx"), None),
            P(("groups", "ctx"), None),
            P(("groups", "ctx"), None),
            P("ctx", None, None),
        ),
        out_specs=(P(("groups", "ctx"), None), P(("groups", "ctx"), None)),
        check_vma=False,
    )
```

```python
import functools
import math

import jax
import jax.numpy as jnp
from jax import lax
from jax.experimental import pallas as pl
from jax.experimental.pallas import tpu as pltpu
from jax.sharding import PartitionSpec as P

H = 64
DL = 512
DR = 64
DV = 128
HI = 32
DI = 128
BLK = 128
WIN = 8
STEP = 32
AT_ONCE = 2
DQ = DL + DR
PACK = DI + DQ

exponent_scale = 192.0 ** (-0.5) * math.log2(math.e)
f32 = jnp.float32
bf16 = jnp.bfloat16
SMALL = pl.CostEstimate(flops=1, bytes_accessed=1, transcendentals=0)


def sort_kernel(order_ref, q_ref, out_ref):
    windows = out_ref.shape[0]
    heads = out_ref.shape[1] // WIN
    rows = jnp.dot(order_ref[...], q_ref[...], preferred_element_type=f32)
    parts = [rows[:, h * DQ : (h + 1) * DQ].reshape(windows, WIN, DQ) for h in range(heads)]
    out_ref[...] = jnp.concatenate(parts, axis=1).astype(bf16)


def sort_queries(order, queries):
    count = queries.shape[0]
    step = 16
    return pl.pallas_call(
        sort_kernel,
        grid=(H // step,),
        in_specs=[
            pl.BlockSpec((count, count), lambda i: (0, 0)),
            pl.BlockSpec((count, step * DQ), lambda i: (0, i)),
        ],
        out_specs=pl.BlockSpec((count // WIN, step * WIN, DQ), lambda i: (0, i, 0)),
        out_shape=jax.ShapeDtypeStruct((count // WIN, H * WIN, DQ), bf16),
        compiler_params=pltpu.CompilerParams(vmem_limit_bytes=36 * 2**20),
        cost_estimate=SMALL,
        name="sort_queries",
    )(order, queries)


def with_block(pieces, place, use):
    size = pieces[0].shape[0]
    if len(pieces) == 1:
        use(pieces[0].at[place])
        return
    for k, piece in enumerate(pieces):

        @pl.when(place // size == k)
        def _():
            use(piece.at[lax.rem(place, size)])


def place_of(relative, j, me):
    if not relative:
        return j
    other = j ^ me
    return (other & 1) * 8 + ((other >> 1) & 1) * 4 + (other >> 2)


def attend_kernel(relative, count, run_ref, offset_ref, key_ref, me_ref, q_ref, pos_ref, keys_ref, *refs):
    pieces = refs[:count]
    out_ref, rhs_ref, acc_ref = refs[count:]
    step = pl.program_id(0)
    me = me_ref[0]

    def load(n, j, column):
        def use(block):
            rhs_ref[n, :, column : column + BLK] = block[DI:PACK, :]

        with_block(pieces, place_of(relative, j, me), use)

    @pl.when(step == 0)
    def _():
        for n in range(AT_ONCE):
            load(n, me, 0)

    column = lax.broadcasted_iota(jnp.int32, (WIN, 2 * BLK), 1)
    last = jnp.where(me > 0, 2 * BLK, 0)
    begin, end = offset_ref[step], offset_ref[step + 1]

    def body(i, carry):
        windows, rows, weights = [], [], []
        for n in range(AT_ONCE):
            token = run_ref[jnp.minimum(begin + i * AT_ONCE + n, end - 1)]
            j = key_ref[token]
            load(n, j, BLK)
            w = token // WIN - step * (STEP // WIN)
            tokens = pl.ds(pl.multiple_of(w * WIN, WIN), WIN)
            usable = (column <= pos_ref[tokens]) | ((column >= BLK) & (column < last))
            windows.append((w, (keys_ref[tokens] == j)[None]))
            scores = jnp.dot(q_ref[w], rhs_ref[n], preferred_element_type=f32)
            bias = jnp.where(usable, 0.0, -jnp.inf).astype(f32)
            rows.append(scores.reshape(H, WIN, 2 * BLK) + bias[None])
        for scores in rows:
            top = jnp.max(scores, axis=-1, keepdims=True)
            expd = jnp.exp2((scores - top) * exponent_scale)
            total = jnp.sum(expd, axis=-1, keepdims=True)
            weights.append((expd * (1.0 / total)).reshape(H * WIN, 2 * BLK).astype(bf16))
        values = [
            lax.dot_general(
                weights[n], rhs_ref[n, 0:DL, :], (((1,), (1,)), ((), ())), preferred_element_type=f32
            )
            for n in range(AT_ONCE)
        ]
        for n, (w, mine) in enumerate(windows):
            old = acc_ref[w].reshape(H, WIN, DL)
            acc_ref[w] = jnp.where(mine, values[n].reshape(H, WIN, DL), old).reshape(H * WIN, DL)
        return carry

    lax.fori_loop(0, (end - begin + AT_ONCE - 1) // AT_ONCE, body, 0)
    for w in range(0, STEP // WIN, 2):
        pair = [acc_ref[w + k].reshape(H, WIN, DL) for k in range(2)]
        out_ref[:, w * WIN : (w + 2) * WIN] = jnp.concatenate(pair, axis=1).astype(bf16)


def runs_of(sorted_key):
    count = sorted_key.shape[0]
    token = jnp.arange(count, dtype=jnp.int32)
    starts = (token % WIN == 0) | (sorted_key != jnp.roll(sorted_key, 1))
    upto = jnp.sum((starts[None, :] & (token[None, :] <= token[:, None])).astype(jnp.int32), axis=1)
    run = jnp.sum((upto[None, :] <= token[:, None]).astype(jnp.int32), axis=1)
    first_token = STEP * jnp.arange(count // STEP + 1, dtype=jnp.int32)
    offset = jnp.sum((starts[None, :] & (token[None, :] < first_token[:, None])).astype(jnp.int32), axis=1)
    return run, offset


def attend(relative, run, offset, sorted_key, me, sorted_q, pieces, pos_column, key_column):
    count = sorted_key.shape[0]
    blocks = sum(p.shape[0] for p in pieces)
    spec = pltpu.PrefetchScalarGridSpec(
        num_scalar_prefetch=4,
        grid=(count // STEP,),
        in_specs=[
            pl.BlockSpec((STEP // WIN, H * WIN, DQ), lambda w, *_: (w, 0, 0)),
            pl.BlockSpec((STEP, 1), lambda w, *_: (w, 0)),
            pl.BlockSpec((STEP, 1), lambda w, *_: (w, 0)),
        ]
        + [pl.BlockSpec((p.shape[0], PACK, BLK), lambda w, *_: (0, 0, 0)) for p in pieces],
        out_specs=pl.BlockSpec((H, STEP, DL), lambda w, *_: (0, w, 0)),
        scratch_shapes=[
            pltpu.VMEM((AT_ONCE, DQ, 2 * BLK), bf16),
            pltpu.VMEM((STEP // WIN, H * WIN, DL), f32),
        ],
    )
    return pl.pallas_call(
        functools.partial(attend_kernel, relative, len(pieces)),
        grid_spec=spec,
        out_shape=jax.ShapeDtypeStruct((H, count, DL), bf16),
        compiler_params=pltpu.CompilerParams(vmem_limit_bytes=(20 + blocks // 2) * 2**20),
        cost_estimate=SMALL,
        name="attend",
    )(run, offset, sorted_key, me, sorted_q, pos_column, key_column, *pieces)


def unit_place(unit, me_ref):
    device, half, relative = unit
    side = (me_ref[1] ^ half) if relative else half
    return (me_ref[0] ^ device) * 2 + side


def project_kernel(units, sizes, before_units, final, me_ref, *refs):
    back_ref = refs[0]
    latents = refs[1 : 1 + len(units)]
    pieces = refs[1 + len(units) : 1 + len(units) + len(sizes)]
    out_ref = refs[-1]
    if before_units:
        before_ref = refs[-2]
        for n, unit in enumerate(before_units):
            place = pl.multiple_of(unit_place(unit, me_ref) * 2 * DV, 2 * DV)
            out_ref[:, pl.ds(place, 2 * DV)] = before_ref[:, n * 2 * DV : (n + 1) * 2 * DV]
    n = 0
    parts = []
    for piece, size in zip(pieces, sizes):
        for k in range(size):
            parts.append(
                jnp.dot(latents[n // 2][n % 2], piece[k], preferred_element_type=f32).astype(bf16)
            )
            n += 1
    rows = jnp.dot(
        back_ref[...], jnp.concatenate(parts, axis=1), preferred_element_type=f32
    ).astype(bf16)
    if not final:
        out_ref[...] = rows
        return
    for n, unit in enumerate(units):
        place = pl.multiple_of(unit_place(unit, me_ref) * 2 * DV, 2 * DV)
        out_ref[:, pl.ds(place, 2 * DV)] = rows[:, n * 2 * DV : (n + 1) * 2 * DV]


def project(me, back, latents, units, pieces, before_units=(), before=None, final=False):
    count = latents.shape[1]
    sizes = tuple(p.shape[0] for p in pieces)
    width = H * DV if final else len(units) * 2 * DV

    def latent_spec(unit):
        return pl.BlockSpec((2, count, DL), lambda i, me_ref: (unit_place(unit, me_ref), 0, 0))

    in_specs = [pl.BlockSpec((count, count), lambda i, m: (0, 0))]
    in_specs += [latent_spec(unit) for unit in units]
    in_specs += [pl.BlockSpec((n, DL, DV), lambda i, m: (0, 0, 0)) for n in sizes]
    operands = [me, back] + [latents] * len(units) + list(pieces)
    if before is not None:
        in_specs.append(pl.BlockSpec(before.shape, lambda i, m: (0, 0)))
        operands.append(before)
    spec = pltpu.PrefetchScalarGridSpec(
        num_scalar_prefetch=1,
        grid=(1,),
        in_specs=in_specs,
        out_specs=pl.BlockSpec((count, width), lambda i, m: (0, 0)),
    )
    return pl.pallas_call(
        functools.partial(project_kernel, tuple(units), sizes, tuple(before_units), final),
        grid_spec=spec,
        out_shape=jax.ShapeDtypeStruct((count, width), bf16),
        compiler_params=pltpu.CompilerParams(vmem_limit_bytes=36 * 2**20),
        cost_estimate=SMALL,
        name="project",
    )(*operands)


def index_kernel(relative, count, me_ref, q_ref, w_ref, *refs):
    pieces = refs[:count]
    out_ref, acc_ref, keys_ref = refs[count:]
    me = me_ref[0]
    rows = q_ref.shape[0]
    acc_ref[...] = jnp.zeros_like(acc_ref)
    row = lax.broadcasted_iota(jnp.int32, (BLK, rows), 0)
    col = lax.broadcasted_iota(jnp.int32, (BLK, rows), 1)

    def block(j, mask):
        def use(piece):
            keys_ref[...] = piece[...]

        with_block(pieces, place_of(relative, j, me), use)
        keys = keys_ref[...]
        total = jnp.zeros((8, rows), f32)
        for h in range(0, HI, 2):
            pair = jnp.concatenate(
                [q_ref[:, h * DI : (h + 1) * DI], q_ref[:, (h + 1) * DI : (h + 2) * DI]], axis=0
            )
            logits = lax.dot_general(keys, pair, (((1,), (1,)), ((), ())), preferred_element_type=f32)
            active = jnp.maximum(logits, 0.0)
            for k in range(2):
                half = active[:, k * rows : (k + 1) * rows]
                if mask is not None:
                    half = jnp.where(mask, half, 0.0)
                sums = jnp.sum(half.reshape(BLK // 8, 8, rows), axis=0)
                total = total + sums * w_ref[h + k : h + k + 1, :]
        acc_ref[pl.ds(j, 1), :] = jnp.sum(total, axis=0, keepdims=True)

    def step(j, carry):
        block(j, None)
        return carry

    lax.fori_loop(0, me, step, 0)
    block(me, row <= col)
    blocks = out_ref.shape[0]
    sums = acc_ref[...]
    position = me * BLK + lax.broadcasted_iota(jnp.int32, (blocks, rows), 1)
    block_first = BLK * lax.broadcasted_iota(jnp.int32, (blocks, rows), 0)
    counts = jnp.clip(position - block_first + 1, 1, BLK).astype(f32)
    out_ref[...] = sums * (DI ** (-0.5)) / counts


def index_scores(relative, me, idx_queries, weights_t, pieces):
    count = idx_queries.shape[0]
    blocks = sum(p.shape[0] for p in pieces)
    spec = pltpu.PrefetchScalarGridSpec(
        num_scalar_prefetch=1,
        grid=(1,),
        in_specs=[
            pl.BlockSpec((count, HI * DI), lambda i, *_: (0, 0)),
            pl.BlockSpec((HI, count), lambda i, *_: (0, 0)),
        ]
        + [pl.BlockSpec((p.shape[0], BLK, DI), lambda i, *_: (0, 0, 0)) for p in pieces],
        out_specs=pl.BlockSpec((blocks, count), lambda i, *_: (0, 0)),
        scratch_shapes=[pltpu.VMEM((blocks, count), f32), pltpu.VMEM((BLK, DI), bf16)],
    )
    return pl.pallas_call(
        functools.partial(index_kernel, relative, len(pieces)),
        grid_spec=spec,
        out_shape=jax.ShapeDtypeStruct((blocks, count), f32),
        compiler_params=pltpu.CompilerParams(vmem_limit_bytes=(12 + blocks // 8) * 2**20),
        cost_estimate=SMALL,
        name="index_scores",
    )(me, idx_queries, weights_t, *pieces).T


def on_ctx(me_to, devices=16):
    return [(i, me_to(i)) for i in range(devices)]


def over_z(k):
    return on_ctx(lambda i: i ^ (4 * k))


OVER_Y = on_ctx(lambda i: i ^ 2)
OVER_CORE = on_ctx(lambda i: i ^ 1)
OVER_XY = [(g * 16 + i, (1 - g) * 16 + (i ^ 2)) for g in range(2) for i in range(16)]


def along(array, pairs):
    return lax.ppermute(array, "ctx", pairs)


def after(array, *others):
    return lax.optimization_barrier((array,) + others)[0]


def on_device(queries, kv_cache, idx_queries, idx_keys, idx_weights, selected, value_maps):
    count = queries.shape[0]
    devices = lax.axis_size("ctx")
    blocks = count * devices // BLK
    assert count == BLK
    me = lax.axis_index("ctx")
    x = lax.axis_index("groups")
    meta = jnp.stack([me, x]).astype(jnp.int32)
    pack = jnp.concatenate([idx_keys, kv_cache.T], axis=0)
    relative = devices == 16 and lax.axis_size("groups") == 2 and value_maps.shape[0] == 4

    if relative:
        half = lax.dynamic_slice_in_dim(value_maps, 2 * x, 2, 0)
        pack_1, pack_2 = along(pack, over_z(1)), along(pack, over_z(2))
        half_1, half_2 = along(half, over_z(1)), along(half, over_z(2))
        from_y = along(value_maps, OVER_Y)
        pack_3 = along(pack_2, over_z(1))
        column_parts = [pack, pack_1, pack_2, pack_3]

    key = jnp.where(me > 0, selected[:, 1], 0)
    token = jnp.arange(count, dtype=jnp.int32)
    before = (key[:, None] < key[None, :]) | ((key[:, None] == key[None, :]) & (token[:, None] < token[None, :]))
    rank = jnp.sum(before.astype(jnp.int32), axis=0)
    order = rank[None, :] == token[:, None]
    back = order.T.astype(bf16)
    sorted_key = jnp.sum(jnp.where(order, key[None, :], 0), axis=1)
    sorted_pos = jnp.sum(jnp.where(order, token[None, :], 0), axis=1)
    run, offset = runs_of(sorted_key)
    pos_column, key_column = sorted_pos[:, None], sorted_key[:, None]
    order = order.astype(bf16)
    if relative:
        columns = (pos_column, key_column)
        order, run, offset, meta, columns, _ = lax.optimization_barrier((order, run, offset, meta, columns, pack_2))
        pos_column, key_column = columns
    sorted_q = sort_queries(order, queries)

    if not relative:
        cache = lax.all_gather(pack, "ctx", axis=0, tiled=True).reshape(blocks, PACK, BLK)
        maps = lax.all_gather(value_maps, "ctx", axis=0, tiled=True)
        scores = index_scores(False, meta, idx_queries, idx_weights.T, [cache])
        latents = attend(False, run, offset, sorted_key, meta, sorted_q, [cache], pos_column, key_column)
        meta = jnp.zeros_like(meta)
        parts = []
        for h in range(0, H, 16):
            units = [(u // 2, u % 2, False) for u in range(h // 2, h // 2 + 8)]
            parts.append(project(meta, back, latents, units, [maps[h : h + 16]]))
        return (jnp.concatenate(parts, axis=1), scores)

    half_3 = along(half_2, over_z(1))
    quarter_parts = [half_1, half_2, half_3]
    column = after(jnp.concatenate(column_parts, axis=0), sorted_q, half_1, half_2, from_y, run, offset, meta, columns)
    column_y = along(column, OVER_Y)
    quarter = jnp.concatenate(quarter_parts, axis=0)
    quarter_x = lax.ppermute(quarter, "groups", [(0, 1), (1, 0)])
    quarter_y = along(quarter, OVER_Y)
    quarter_xy = lax.ppermute(quarter, ("groups", "ctx"), OVER_XY)
    pieces = [column, column_y, along(column, OVER_CORE), along(after(column_y, half_3), OVER_CORE)]
    pieces = [p.reshape(4, PACK, BLK) for p in pieces]
    pieces, quarter = lax.optimization_barrier((pieces, quarter))

    latents = attend(True, run, offset, sorted_key, meta, sorted_q, pieces, pos_column, key_column)
    latents, quarter_x, quarter_y, quarter_xy = lax.optimization_barrier(
        (latents, quarter_x, quarter_y, quarter_xy)
    )
    scores = index_scores(True, meta, idx_queries, idx_weights.T, pieces)

    def both_cores(arrays, units):
        arrays = list(arrays) + [along(a, OVER_CORE) for a in arrays]
        return arrays, units + [(device ^ 1, half, rel) for device, half, rel in units]

    early, early_units = both_cores(
        [value_maps, from_y, quarter],
        [(0, 0, False), (0, 1, False), (2, 0, False), (2, 1, False)] + [(4 * z, 0, True) for z in (1, 2, 3)],
    )
    early_out = project(meta, back, latents, early_units, early)
    late_in = [quarter_x, quarter_y, quarter_xy]
    late, late_units = both_cores(
        late_in,
        [(4 * z, 1, True) for z in (1, 2, 3)]
        + [(4 * z + 2, 0, True) for z in (1, 2, 3)]
        + [(4 * z + 2, 1, True) for z in (1, 2, 3)],
    )
    attended = project(meta, back, latents, late_units, late, early_units, early_out, final=True)
    return (attended, scores)


def solution(mesh):
    return jax.shard_map(
        on_device,
        mesh=mesh,
        in_specs=(
            P(("groups", "ctx"), None),
            P(("groups", "ctx"), None),
            P(("groups", "ctx"), None),
            P(("groups", "ctx"), None),
            P(("groups", "ctx"), None),
            P(("groups", "ctx"), None),
            P("ctx", None, None),
        ),
        out_specs=(P(("groups", "ctx"), None), P(("groups", "ctx"), None)),
        check_vma=False,
    )
```

```python
import functools
import math

import jax
import jax.numpy as jnp
from jax import lax
from jax.experimental import pallas as pl
from jax.experimental.pallas import tpu as pltpu
from jax.sharding import PartitionSpec as P

H = 64
DL = 512
DR = 64
DV = 128
HI = 32
DI = 128
BLK = 128
WIN = 8
STEP = 64
AT_ONCE = 2
DQ = DL + DR
PACK = DI + DQ

exponent_scale = 192.0 ** (-0.5) * math.log2(math.e)
f32 = jnp.float32
bf16 = jnp.bfloat16
SMALL = pl.CostEstimate(flops=1, bytes_accessed=1, transcendentals=0)


def sort_kernel(order_ref, q_ref, out_ref):
    windows = out_ref.shape[0]
    heads = out_ref.shape[1] // WIN
    rows = jnp.dot(order_ref[...], q_ref[...], preferred_element_type=f32)
    parts = [rows[:, h * DQ : (h + 1) * DQ].reshape(windows, WIN, DQ) for h in range(heads)]
    out_ref[...] = jnp.concatenate(parts, axis=1).astype(bf16)


def sort_queries(order, queries):
    count = queries.shape[0]
    step = 16
    return pl.pallas_call(
        sort_kernel,
        grid=(H // step,),
        in_specs=[
            pl.BlockSpec((count, count), lambda i: (0, 0)),
            pl.BlockSpec((count, step * DQ), lambda i: (0, i)),
        ],
        out_specs=pl.BlockSpec((count // WIN, step * WIN, DQ), lambda i: (0, i, 0)),
        out_shape=jax.ShapeDtypeStruct((count // WIN, H * WIN, DQ), bf16),
        compiler_params=pltpu.CompilerParams(vmem_limit_bytes=36 * 2**20),
        cost_estimate=SMALL,
        name="sort_queries",
    )(order, queries)


def with_block(pieces, place, use):
    size = pieces[0].shape[0]
    if len(pieces) == 1:
        use(pieces[0].at[place])
        return
    for k, piece in enumerate(pieces):

        @pl.when(place // size == k)
        def _():
            use(piece.at[lax.rem(place, size)])


def place_of(relative, j, me):
    if not relative:
        return j
    other = j ^ me
    return (other & 1) * 8 + ((other >> 1) & 1) * 4 + (other >> 2)


def attend_kernel(relative, count, run_ref, offset_ref, key_ref, me_ref, q_ref, pos_ref, keys_ref, *refs):
    pieces = refs[:count]
    out_ref, rhs_ref, acc_ref = refs[count:]
    step = pl.program_id(0)
    me = me_ref[0]

    def load(n, j, column):
        def use(block):
            rhs_ref[n, :, column : column + BLK] = block[...]

        with_block(pieces, place_of(relative, j, me), use)

    @pl.when(step == 0)
    def _():
        for n in range(AT_ONCE):
            load(n, me, 0)

    column = lax.broadcasted_iota(jnp.int32, (WIN, 2 * BLK), 1)
    last = jnp.where(me > 0, 2 * BLK, 0)
    begin, end = offset_ref[step], offset_ref[step + 1]

    def body(i, carry):
        windows, rows, weights = [], [], []
        for n in range(AT_ONCE):
            token = run_ref[jnp.minimum(begin + i * AT_ONCE + n, end - 1)]
            j = key_ref[token]
            load(n, j, BLK)
            w = token // WIN - step * (STEP // WIN)
            tokens = pl.ds(pl.multiple_of(w * WIN, WIN), WIN)
            usable = (column <= pos_ref[tokens][:, 0:1]) | ((column >= BLK) & (column < last))
            windows.append((w, (keys_ref[tokens][:, 0:1] == j)[None]))
            scores = jnp.dot(q_ref[w], rhs_ref[n], preferred_element_type=f32)
            bias = jnp.where(usable, 0.0, -jnp.inf).astype(f32)
            rows.append(scores.reshape(H, WIN, 2 * BLK) + bias[None])
        for scores in rows:
            top = jnp.max(scores, axis=-1, keepdims=True)
            expd = jnp.exp2((scores - top) * exponent_scale)
            total = jnp.sum(expd, axis=-1, keepdims=True)
            weights.append((expd * (1.0 / total)).reshape(H * WIN, 2 * BLK).astype(bf16))
        values = [
            lax.dot_general(
                weights[n], rhs_ref[n, 0:DL, :], (((1,), (1,)), ((), ())), preferred_element_type=f32
            )
            for n in range(AT_ONCE)
        ]
        for n, (w, mine) in enumerate(windows):
            old = acc_ref[w].reshape(H, WIN, DL)
            acc_ref[w] = jnp.where(mine, values[n].reshape(H, WIN, DL), old).reshape(H * WIN, DL)
        return carry

    lax.fori_loop(0, (end - begin + AT_ONCE - 1) // AT_ONCE, body, 0)
    for w in range(0, STEP // WIN, 2):
        pair = [acc_ref[w + k].reshape(H, WIN, DL) for k in range(2)]
        out_ref[:, w * WIN : (w + 2) * WIN] = jnp.concatenate(pair, axis=1).astype(bf16)


def runs_of(sorted_key):
    count = sorted_key.shape[0]
    token = jnp.arange(count, dtype=jnp.int32)
    starts = (token % WIN == 0) | (sorted_key != jnp.roll(sorted_key, 1))
    upto = jnp.sum((starts[None, :] & (token[None, :] <= token[:, None])).astype(jnp.int32), axis=1)
    run = jnp.sum((upto[None, :] <= token[:, None]).astype(jnp.int32), axis=1)
    first_token = STEP * jnp.arange(count // STEP + 1, dtype=jnp.int32)
    offset = jnp.sum((starts[None, :] & (token[None, :] < first_token[:, None])).astype(jnp.int32), axis=1)
    return run, offset


def attend(relative, run, offset, sorted_key, me, sorted_q, pieces, pos_column, key_column):
    count = sorted_key.shape[0]
    blocks = sum(p.shape[0] for p in pieces)
    spec = pltpu.PrefetchScalarGridSpec(
        num_scalar_prefetch=4,
        grid=(count // STEP,),
        in_specs=[
            pl.BlockSpec((STEP // WIN, H * WIN, DQ), lambda w, *_: (w, 0, 0)),
            pl.BlockSpec((STEP, BLK), lambda w, *_: (w, 0)),
            pl.BlockSpec((STEP, BLK), lambda w, *_: (w, 0)),
        ]
        + [pl.BlockSpec((p.shape[0], DQ, BLK), lambda w, *_: (0, 0, 0)) for p in pieces],
        out_specs=pl.BlockSpec((H, STEP, DL), lambda w, *_: (0, w, 0)),
        scratch_shapes=[
            pltpu.VMEM((AT_ONCE, DQ, 2 * BLK), bf16),
            pltpu.VMEM((STEP // WIN, H * WIN, DL), f32),
        ],
    )
    return pl.pallas_call(
        functools.partial(attend_kernel, relative, len(pieces)),
        grid_spec=spec,
        out_shape=jax.ShapeDtypeStruct((H, count, DL), bf16),
        compiler_params=pltpu.CompilerParams(vmem_limit_bytes=(30 + blocks // 2) * 2**20),
        cost_estimate=SMALL,
        name="attend",
    )(run, offset, sorted_key, me, sorted_q, pos_column, key_column, *pieces)


def unit_place(unit, me_ref):
    device, half, relative = unit
    side = (me_ref[1] ^ half) if relative else half
    return (me_ref[0] ^ device) * 2 + side


def project_kernel(units, sizes, before_units, final, me_ref, *refs):
    back_ref = refs[0]
    latents = refs[1 : 1 + len(units)]
    pieces = refs[1 + len(units) : 1 + len(units) + len(sizes)]
    out_ref = refs[-1]
    if before_units:
        before_ref = refs[-2]
        for n, unit in enumerate(before_units):
            place = pl.multiple_of(unit_place(unit, me_ref) * 2 * DV, 2 * DV)
            out_ref[:, pl.ds(place, 2 * DV)] = before_ref[:, n * 2 * DV : (n + 1) * 2 * DV]
    n = 0
    parts = []
    for piece, size in zip(pieces, sizes):
        for k in range(size):
            parts.append(
                jnp.dot(latents[n // 2][n % 2], piece[k], preferred_element_type=f32).astype(bf16)
            )
            n += 1
    rows = jnp.dot(
        back_ref[...], jnp.concatenate(parts, axis=1), preferred_element_type=f32
    ).astype(bf16)
    if not final:
        out_ref[...] = rows
        return
    for n, unit in enumerate(units):
        place = pl.multiple_of(unit_place(unit, me_ref) * 2 * DV, 2 * DV)
        out_ref[:, pl.ds(place, 2 * DV)] = rows[:, n * 2 * DV : (n + 1) * 2 * DV]


def project(me, back, latents, units, pieces, before_units=(), before=None, final=False):
    count = latents.shape[1]
    sizes = tuple(p.shape[0] for p in pieces)
    width = H * DV if final else len(units) * 2 * DV

    def latent_spec(unit):
        return pl.BlockSpec((2, count, DL), lambda i, me_ref: (unit_place(unit, me_ref), 0, 0))

    in_specs = [pl.BlockSpec((count, count), lambda i, m: (0, 0))]
    in_specs += [latent_spec(unit) for unit in units]
    in_specs += [pl.BlockSpec((n, DL, DV), lambda i, m: (0, 0, 0)) for n in sizes]
    operands = [me, back] + [latents] * len(units) + list(pieces)
    if before is not None:
        in_specs.append(pl.BlockSpec(before.shape, lambda i, m: (0, 0)))
        operands.append(before)
    spec = pltpu.PrefetchScalarGridSpec(
        num_scalar_prefetch=1,
        grid=(1,),
        in_specs=in_specs,
        out_specs=pl.BlockSpec((count, width), lambda i, m: (0, 0)),
    )
    return pl.pallas_call(
        functools.partial(project_kernel, tuple(units), sizes, tuple(before_units), final),
        grid_spec=spec,
        out_shape=jax.ShapeDtypeStruct((count, width), bf16),
        compiler_params=pltpu.CompilerParams(vmem_limit_bytes=36 * 2**20),
        cost_estimate=SMALL,
        name="project",
    )(*operands)


def index_kernel(relative, count, me_ref, q_ref, w_ref, *refs):
    pieces = refs[:count]
    out_ref, acc_ref, keys_ref = refs[count:]
    me = me_ref[0]
    rows = q_ref.shape[0]
    acc_ref[...] = jnp.zeros_like(acc_ref)
    row = lax.broadcasted_iota(jnp.int32, (BLK, rows), 0)
    col = lax.broadcasted_iota(jnp.int32, (BLK, rows), 1)

    def block(j, mask):
        def use(piece):
            keys_ref[...] = piece[...]

        with_block(pieces, place_of(relative, j, me), use)
        keys = keys_ref[...]
        total = jnp.zeros((8, rows), f32)
        for h in range(0, HI, 2):
            pair = jnp.concatenate(
                [q_ref[:, h * DI : (h + 1) * DI], q_ref[:, (h + 1) * DI : (h + 2) * DI]], axis=0
            )
            logits = lax.dot_general(keys, pair, (((1,), (1,)), ((), ())), preferred_element_type=f32)
            active = jnp.maximum(logits, 0.0)
            for k in range(2):
                half = active[:, k * rows : (k + 1) * rows]
                if mask is not None:
                    half = jnp.where(mask, half, 0.0)
                sums = jnp.sum(half.reshape(BLK // 8, 8, rows), axis=0)
                total = total + sums * w_ref[h + k : h + k + 1, :]
        acc_ref[pl.ds(j, 1), :] = jnp.sum(total, axis=0, keepdims=True)

    def step(j, carry):
        block(j, None)
        return carry

    lax.fori_loop(0, me, step, 0)
    block(me, row <= col)
    blocks = out_ref.shape[0]
    sums = acc_ref[...]
    position = me * BLK + lax.broadcasted_iota(jnp.int32, (blocks, rows), 1)
    block_first = BLK * lax.broadcasted_iota(jnp.int32, (blocks, rows), 0)
    counts = jnp.clip(position - block_first + 1, 1, BLK).astype(f32)
    out_ref[...] = sums * (DI ** (-0.5)) / counts


def index_scores(relative, me, idx_queries, weights_t, pieces):
    count = idx_queries.shape[0]
    blocks = sum(p.shape[0] for p in pieces)
    spec = pltpu.PrefetchScalarGridSpec(
        num_scalar_prefetch=1,
        grid=(1,),
        in_specs=[
            pl.BlockSpec((count, HI * DI), lambda i, *_: (0, 0)),
            pl.BlockSpec((HI, count), lambda i, *_: (0, 0)),
        ]
        + [pl.BlockSpec((p.shape[0], BLK, DI), lambda i, *_: (0, 0, 0)) for p in pieces],
        out_specs=pl.BlockSpec((blocks, count), lambda i, *_: (0, 0)),
        scratch_shapes=[pltpu.VMEM((blocks, count), f32), pltpu.VMEM((BLK, DI), bf16)],
    )
    return pl.pallas_call(
        functools.partial(index_kernel, relative, len(pieces)),
        grid_spec=spec,
        out_shape=jax.ShapeDtypeStruct((blocks, count), f32),
        compiler_params=pltpu.CompilerParams(vmem_limit_bytes=(12 + blocks // 8) * 2**20),
        cost_estimate=SMALL,
        name="index_scores",
    )(me, idx_queries, weights_t, *pieces).T


def on_ctx(me_to, devices=16):
    return [(i, me_to(i)) for i in range(devices)]


def over_z(k):
    return on_ctx(lambda i: i ^ (4 * k))


OVER_Y = on_ctx(lambda i: i ^ 2)
OVER_CORE = on_ctx(lambda i: i ^ 1)
OVER_XY = [(g * 16 + i, (1 - g) * 16 + (i ^ 2)) for g in range(2) for i in range(16)]


def along(array, pairs):
    return lax.ppermute(array, "ctx", pairs)


def across(array):
    return lax.ppermute(array, "groups", [(0, 1), (1, 0)])


def after(array, *others):
    return lax.optimization_barrier((array,) + others)[0]


def on_device(queries, kv_cache, idx_queries, idx_keys, idx_weights, selected, value_maps):
    count = queries.shape[0]
    devices = lax.axis_size("ctx")
    blocks = count * devices // BLK
    assert count == BLK
    me = lax.axis_index("ctx")
    x = lax.axis_index("groups")
    meta = jnp.stack([me, x]).astype(jnp.int32)
    pack = jnp.concatenate([idx_keys, kv_cache.T], axis=0)
    relative = devices == 16 and lax.axis_size("groups") == 2 and value_maps.shape[0] == 4

    if relative:
        half = lax.dynamic_slice_in_dim(value_maps, 2 * x, 2, 0)
        pack_1, pack_2 = along(pack, over_z(1)), along(pack, over_z(2))
        half_1, half_2 = along(half, over_z(1)), along(half, over_z(2))
        from_y = along(value_maps, OVER_Y)
        pack_3 = along(pack_2, over_z(1))
        column_parts = [pack, pack_1, pack_2, pack_3]

    key = jnp.where(me > 0, selected[:, 1], 0)
    token = jnp.arange(count, dtype=jnp.int32)
    before = (key[:, None] < key[None, :]) | ((key[:, None] == key[None, :]) & (token[:, None] < token[None, :]))
    rank = jnp.sum(before.astype(jnp.int32), axis=0)
    order = rank[None, :] == token[:, None]
    back = order.T.astype(bf16)
    sorted_key = jnp.sum(jnp.where(order, key[None, :], 0), axis=1)
    sorted_pos = jnp.sum(jnp.where(order, token[None, :], 0), axis=1)
    run, offset = runs_of(sorted_key)
    pos_column = jnp.broadcast_to(sorted_pos[:, None], (count, BLK))
    key_column = jnp.broadcast_to(sorted_key[:, None], (count, BLK))
    order = order.astype(bf16)
    if relative:
        columns = (pos_column, key_column)
        order, run, offset, meta, columns, _, half_2 = lax.optimization_barrier(
            (order, run, offset, meta, columns, pack_2, half_2)
        )
        pos_column, key_column = columns
    sorted_q = sort_queries(order, queries)

    if not relative:
        cache = lax.all_gather(pack, "ctx", axis=0, tiled=True).reshape(blocks, PACK, BLK)
        maps = lax.all_gather(value_maps, "ctx", axis=0, tiled=True)
        scores = index_scores(False, meta, idx_queries, idx_weights.T, [cache[:, 0:DI]])
        latents = attend(False, run, offset, sorted_key, meta, sorted_q, [cache[:, DI:PACK]], pos_column, key_column)
        meta = jnp.zeros_like(meta)
        parts = []
        for h in range(0, H, 16):
            units = [(u // 2, u % 2, False) for u in range(h // 2, h // 2 + 8)]
            parts.append(project(meta, back, latents, units, [maps[h : h + 16]]))
        return (jnp.concatenate(parts, axis=1), scores)

    half_3 = along(half_2, over_z(1))
    first = jnp.concatenate([half_1, half_2], axis=0)
    first_x, first_y = across(first), along(first, OVER_Y)
    early_keys = jnp.concatenate([p[0:DI] for p in column_parts], axis=0)
    keys_y = along(early_keys, OVER_Y)
    keys_plane = jnp.concatenate([early_keys, keys_y], axis=0)
    keys = [keys_plane, along(keys_plane, OVER_CORE)]
    keys = [p.reshape(8, BLK, DI) for p in keys]
    scores = index_scores(True, meta, idx_queries, idx_weights.T, keys)
    column = jnp.concatenate([p[DI:PACK] for p in column_parts], axis=0)
    column = after(column, sorted_q, first_x, first_y, half_3, from_y, run, offset, meta, columns)
    column_y = along(column, OVER_Y)
    last_y = along(half_3, OVER_Y)
    from_x = across(jnp.concatenate([first_y, half_3], axis=0))
    last_xy = lax.ppermute(half_3, ("groups", "ctx"), OVER_XY)
    early = [value_maps, from_y, first, half_3]
    early_core = [along(a, OVER_CORE) for a in early]
    pieces = [column, column_y, along(column, OVER_CORE), along(after(column_y, scores, early_core), OVER_CORE)]
    pieces = [p.reshape(4, DQ, BLK) for p in pieces]
    first_core = [along(first_x, OVER_CORE), along(first_y, OVER_CORE)]

    latents = attend(True, run, offset, sorted_key, meta, sorted_q, pieces, pos_column, key_column)
    latents, first_core, from_x, last_y, last_xy = lax.optimization_barrier(
        (latents, first_core, from_x, last_y, last_xy)
    )
    late = [from_x, last_y, last_xy]
    late_core = [along(a, OVER_CORE) for a in late]

    early_units = [(0, 0, False), (0, 1, False), (2, 0, False), (2, 1, False)] + [(4 * z, 0, True) for z in (1, 2, 3)]
    early_units = early_units + [(device ^ 1, half, rel) for device, half, rel in early_units]
    early_out = project(meta, back, latents, early_units, early + early_core)
    first_units = [(4 * z, 1, True) for z in (1, 2)] + [(4 * z + 2, 0, True) for z in (1, 2)]
    late_units = [(4 * z + 2, 1, True) for z in (1, 2)] + [(12, 1, True), (14, 0, True), (14, 1, True)]
    units = first_units + late_units
    units = units + [(device ^ 1, half, rel) for device, half, rel in units]
    arrays = [first_x, first_y] + late + first_core + late_core
    attended = project(meta, back, latents, units, arrays, early_units, early_out, final=True)
    return (attended, scores)


def solution(mesh):
    return jax.shard_map(
        on_device,
        mesh=mesh,
        in_specs=(
            P(("groups", "ctx"), None),
            P(("groups", "ctx"), None),
            P(("groups", "ctx"), None),
            P(("groups", "ctx"), None),
            P(("groups", "ctx"), None),
            P(("groups", "ctx"), None),
            P("ctx", None, None),
        ),
        out_specs=(P(("groups", "ctx"), None), P(("groups", "ctx"), None)),
        check_vma=False,
    )
```
